32 devices in a mesh: wall: 8 (over z, x), stream: 4 (over y, core).
Axes of the slice: x: 2, y: 2, z: 4, core: 2. Of those that a mesh axis runs over, the one named last changes fastest.
Arguments:
- dist: float32 [8, 64, 32, 1024], P(None, None, 'stream', 'wall'), may hold values from 0.25 to 4
- quad_weight: float32 [8, 64], replicated, may hold values from 0.0009765625 to 0.00390625
- vel_x: float32 [64], replicated, may hold values from -3 to 3
- vel_y: float32 [8], replicated, may hold values from -3 to 3, as said below
- flags: int32 [32, 1024], P('stream', 'wall'), may hold values from 0 to 2
- block_inverse: float32 [8, 128, 128], replicated, as said below
- line_coupling: float32 [8], replicated, as said below
Outputs:
- advanced: float32 [8, 64, 32, 1024], P(None, None, 'stream', 'wall')
The draws below stay inside these ranges and needn't reach their ends.
Inputs may be any that keep to these rules, and one draw needn't show every extreme that they name: vel_y[g] is positive for g < 4 and negative otherwise. block_inverse[g] is zero above the diagonal for g < 4 and zero below it otherwise; no entry is negative. line_coupling[g] times the entry of block_inverse[g] that links the last node of a block to the first node of the next (row 127, column 0 for g < 4; row 0, column 127 otherwise) is positive and below 1.
All inputs are finite; a program needn't handle non-finite values.
Results may differ from the reference program's by a relative error of at most 0.00023.
Values sent between devices are 32-bit elements; how exact they have to be, the bound alone decides.
A program may use at most 64 MiB of HBM per device.

```python
import math
import jax
import jax.numpy as jnp
from jax import lax

VY = 8
VX = 64
CW = 128
ITERS = 2
NS = 32
NW = 1024


def block_rates(key):
    first_key, second_key = jax.random.split(jax.random.fold_in(key, 11))
    order = jax.random.permutation(first_key, VY)
    slower = order < VY // 2
    spread = jax.random.uniform(second_key, (VY,), jnp.float32)
    keep_block = jnp.where(slower, 0.86 + 0.06 * spread, 0.02 + 0.06 * spread)
    return jnp.exp(jnp.log(keep_block) / CW)


def draw_block_inverse(key, part):
    ratio = block_rates(key)
    rows = jnp.arange(CW)[:, None]
    cols = jnp.arange(CW)[None, :]
    downward = (jnp.arange(VY) < VY // 2)[:, None, None]
    offset = jnp.where(downward, rows - cols, cols - rows)
    inside = offset >= 0
    noise = jax.random.uniform(jax.random.fold_in(key, 23), (VY, CW, CW), jnp.float32, 0.5, 1.5)
    noise = jnp.where(offset == CW - 1, 1.0, noise)
    power = jnp.exp(jnp.maximum(offset, 0).astype(jnp.float32) * jnp.log(ratio)[:, None, None])
    values = (1.0 - ratio)[:, None, None] / 1.3 * power * noise
    return jnp.where(inside, values, 0.0).astype(jnp.float32)


def draw_line_coupling(key, part):
    ratio = block_rates(key)
    factor = jax.random.uniform(jax.random.fold_in(key, 37), (VY,), jnp.float32, 0.9, 1.0)
    return (1.3 * ratio / (1.0 - ratio) * factor).astype(jnp.float32)


def draw_vel_y(key, part):
    magnitude = jax.random.uniform(jax.random.fold_in(key, 41), (VY,), jnp.float32, 0.5, 3.0)
    signed = jnp.where(jnp.arange(VY) < VY // 2, 1.0, -1.0)
    return (signed * magnitude).astype(jnp.float32)


def with_ends(drawn, key, smallest, largest):
    shape = drawn.shape
    index_at = [jax.random.randint(jax.random.fold_in(key, axis), (), 0, shape[axis]) for axis in range(len(shape))]
    drawn = drawn.at[tuple(index_at)].set(smallest)
    longest = shape.index(max(shape))
    index_at[longest] = (index_at[longest] + 1) % shape[longest]
    return drawn.at[tuple(index_at)].set(largest)


def level_of(stream_key, extent, cuts, least, high):
    gain = 1.0
    for dim, shards_of in cuts:
        steps = jax.random.uniform(jax.random.fold_in(jax.random.fold_in(stream_key, 6), dim), (shards_of,), jnp.float32, least / len(cuts), high / len(cuts))
        gain = gain * jnp.repeat(jnp.exp(steps), extent[dim] // shards_of).reshape((-1,) + (1,) * (len(extent) - 1 - dim))
    return gain


def setup_inputs(seed: int = 0) -> dict:
    streams_of = jax.random.split(jax.random.key(seed), 8)
    dist = jnp.clip(jnp.exp(math.log(4.0) - 2.7725887 * jax.random.uniform(streams_of[0], (VY, VX, NS, NW), jnp.float32) ** level_of(streams_of[0], (VY, VX, NS, NW), ((2, 4), (3, 8)), -0.2, 0.2)), 0.25, 4.0)
    quad_weight = jnp.clip(jnp.exp(jax.random.uniform(streams_of[1], (VY, VX), jnp.float32, math.log(0.0009765625), math.log(0.00390625))), 0.0009765625, 0.00390625)
    vel_x = jnp.clip(jax.random.uniform(streams_of[2], (VX,), jnp.float32, -3.0, 3.0), -3.0, 3.0)
    vel_y = draw_vel_y(jax.random.fold_in(streams_of[7], 71), 0)
    flags = with_ends(jax.random.randint(streams_of[4], (NS, NW), 0, 3), jax.random.fold_in(streams_of[4], 1), 0, 2).astype(jnp.int32)
    block_inverse = draw_block_inverse(jax.random.fold_in(streams_of[7], 71), 0)
    line_coupling = draw_line_coupling(jax.random.fold_in(streams_of[7], 71), 0)
    return dict(dist=dist, quad_weight=quad_weight, vel_x=vel_x, vel_y=vel_y, flags=flags, block_inverse=block_inverse, line_coupling=line_coupling)


CFL_STREAM = 0.12
RELAX = 0.3
PENALTY = 0.5
INLET_SPEED = 0.5


def maxwell_tables(quad_weight, vel_x, vel_y):
    square_y = vel_y[:, None] * vel_y[:, None]
    rest_table = jnp.exp(-(vel_x[None, :] * vel_x[None, :] + square_y) / 2.0)
    shifted = vel_x[None, :] - INLET_SPEED
    inlet_table = jnp.exp(-(shifted * shifted + square_y) / 2.0)
    rest_table = rest_table / jnp.sum(quad_weight * rest_table)
    inlet_table = inlet_table / jnp.sum(quad_weight * inlet_table)
    return rest_table, inlet_table


def line_solve(rhs, inverse, coupling, downward):
    highest = lax.Precision.HIGHEST
    block_len = inverse.shape[0]
    blocks = rhs.reshape(rhs.shape[0], rhs.shape[1], -1, block_len)
    solved = jnp.einsum("xsbj,ij->xsbi", blocks, inverse, precision=highest)
    if downward:
        ends = solved[..., block_len - 1]
        factor = coupling * inverse[block_len - 1, 0]
        spike = coupling * inverse[:, 0]
    else:
        ends = solved[..., 0]
        factor = coupling * inverse[0, block_len - 1]
        spike = coupling * inverse[:, block_len - 1]

    def advance(carry, entry):
        return entry + factor * carry, carry

    _, before = lax.scan(advance, jnp.zeros_like(ends[:, :, 0]), jnp.moveaxis(ends, 2, 0), reverse=not downward)
    before = jnp.moveaxis(before, 0, 2)
    result = solved + spike * before[..., None]
    return result.reshape(rhs.shape)


def reference(dist, quad_weight, vel_x, vel_y, flags, block_inverse, line_coupling):
    highest = lax.Precision.HIGHEST
    half_groups = VY // 2
    rest_table, inlet_table = maxwell_tables(quad_weight, vel_x, vel_y)
    solid = (flags == 1).astype(jnp.float32)
    inflow = (flags == 2).astype(jnp.float32)
    moment_table = jnp.stack([quad_weight, quad_weight * vel_x[None, :], quad_weight * vel_y[:, None]])
    speed_column = vel_x[:, None, None]
    current = dist
    for sweep in range(ITERS):
        moments = jnp.einsum("mgx,gxsw->msw", moment_table, current, precision=highest)
        density = moments[0]
        speed_x = moments[1] / density
        speed_y = moments[2] / density

        def exponent(group):
            diff_x = speed_column - speed_x[None]
            diff_y = vel_y[group] - speed_y[None]
            return jnp.exp(-(diff_x * diff_x + diff_y * diff_y) / 2.0)

        zsum = jnp.zeros_like(density)
        for group in range(VY):
            zsum = zsum + jnp.einsum("x,xsw->sw", quad_weight[group], exponent(group), precision=highest)
        outputs = []
        for group in range(VY):
            equil = density[None] * exponent(group) / zsum[None]
            values = current[group]
            left_side = jnp.roll(values, 1, axis=1)
            right_side = jnp.roll(values, -1, axis=1)
            upwind = jnp.maximum(speed_column, 0.0) * (values - left_side) + jnp.minimum(speed_column, 0.0) * (right_side - values)
            boundary = solid[None] * (density[None] * rest_table[group][:, None, None] - values) + inflow[None] * (inlet_table[group][:, None, None] - values)
            rhs = values - CFL_STREAM * upwind + RELAX * equil + PENALTY * boundary
            outputs.append(line_solve(rhs, block_inverse[group], line_coupling[group], group < half_groups))
        current = jnp.stack(outputs)
    return current
```

```python
import functools
import jax
import jax.numpy as jnp
from jax import lax
from jax.experimental import pallas as pl
from jax.experimental.pallas import tpu as pltpu
from jax.sharding import PartitionSpec as P

ITERS = 2
CFL_STREAM = 0.12
RELAX = 0.3
PENALTY = 0.5
INLET_SPEED = 0.5
MESH = pl.DeviceIdType.MESH
F32 = jnp.float32
BF16 = jnp.bfloat16
NT = (((1,), (1,)), ((), ()))
TN = (((0,), (0,)), ((), ()))


def split(value):
    high = value.astype(BF16)
    return high, (value - high.astype(F32)).astype(BF16)


def kernel(
    groups, nx, ns, n_wall, n_stream,
    dist, qw, vx, vy, flags, inv, lc,
    out,
    cur, rhs, packed, weight, end_row, spike, factor, ex, tx, rx, ix, ry, eya,
    edge_l, edge_r, halo_l, halo_r, ends, others, before,
    load_sem, sl_sem, sr_sem, rl_sem, rr_sem, ws_sem, wr_sem,
):
    cw = cur.shape[1]
    half = groups // 2
    rows = nx * ns
    part = ends.shape[3]
    pieces = rows // part
    wall = lax.axis_index("wall")
    stream = lax.axis_index("stream")
    left = lax.rem(stream + n_stream - 1, n_stream)
    right = lax.rem(stream + 1, n_stream)

    loads = [
        pltpu.make_async_copy(
            dist.at[pl.ds(g * rows, rows)], cur.at[pl.ds(g * rows, rows)], load_sem.at[g]
        )
        for g in range(groups)
    ]
    for load in loads:
        load.start()

    barrier = pltpu.get_barrier_semaphore()
    for to in (left, right):
        pl.semaphore_signal(barrier, inc=1, device_id=(wall, to), device_id_type=MESH)
    for step in range(1, n_wall):
        to = lax.rem(wall + step, n_wall)
        pl.semaphore_signal(barrier, inc=1, device_id=(to, stream), device_id_type=MESH)
    pl.semaphore_wait(barrier, 2 + n_wall - 1)

    def halo_copies(it, g):
        here = pl.ds(g * nx, nx)
        return (
            pltpu.make_async_remote_copy(
                src_ref=edge_r.at[it, here], dst_ref=halo_l.at[it, here],
                send_sem=sr_sem.at[it, g], recv_sem=rl_sem.at[it, g],
                device_id=(wall, right), device_id_type=MESH,
            ),
            pltpu.make_async_remote_copy(
                src_ref=edge_l.at[it, here], dst_ref=halo_r.at[it, here],
                send_sem=sl_sem.at[it, g], recv_sem=rr_sem.at[it, g],
                device_id=(wall, left), device_id_type=MESH,
            ),
        )

    def send_edges(it, g):
        here = pl.ds(g * nx, nx)
        edge_r[it, here, :] = cur[pl.ds(g * rows + ns - 1, nx, stride=ns), :]
        edge_l[it, here, :] = cur[pl.ds(g * rows, nx, stride=ns), :]
        for copy in halo_copies(it, g):
            copy.start()

    for g in range(groups):
        loads[g].wait()
        send_edges(0, g)

    zero = jnp.zeros((ns, cw), F32)

    def table_step(x, carry):
        v = jnp.full((ns, cw), vx[x], F32)
        rest = jnp.exp(-0.5 * (v * v))
        shifted = v - INLET_SPEED
        inlet = jnp.exp(-0.5 * (shifted * shifted))
        rx[x] = rest
        ix[x] = inlet
        sums = list(carry)
        for g in range(groups):
            w = qw[g, x]
            sums[g] = sums[g] + w * rest
            sums[groups + g] = sums[groups + g] + w * inlet
        return tuple(sums)

    sums = lax.fori_loop(0, nx, table_step, (zero,) * (2 * groups))
    rest_sum = zero
    inlet_sum = zero
    for g in range(groups):
        v = jnp.full((ns, cw), vy[g], F32)
        factor_y = jnp.exp(-0.5 * (v * v))
        ry[g] = factor_y
        rest_sum = rest_sum + factor_y * sums[g]
        inlet_sum = inlet_sum + factor_y * sums[groups + g]
    kind = flags[...]
    solid = jnp.where(kind == 1, PENALTY, 0.0).astype(F32)
    inflow = jnp.where(kind == 2, PENALTY, 0.0).astype(F32)
    keep = 1.0 - solid - inflow
    solid_part = solid / rest_sum
    inlet_part = inflow / inlet_sum

    row16 = lax.broadcasted_iota(jnp.int32, (16, cw), 0)
    for g in range(groups):
        m = inv[g]
        high, low = split(m)
        weight[g, 0:cw, 0:cw] = high
        weight[g, 0:cw, cw:] = high
        weight[g, cw:, 0:cw] = low
        weight[g, cw:, cw:] = jnp.zeros((cw, cw), BF16)
        mt = m.T
        down = g < half
        last = m[cw - 1 : cw, :] if down else m[0:1, :]
        col = (mt[0:1, :] if down else mt[cw - 1 : cw, :]) * lc[g]
        last_high, last_low = split(last)
        last_high = last_high.astype(F32)
        last_low = last_low.astype(F32)
        end_row[g, :, 0:cw] = jnp.where(
            row16 == 0, last_high, jnp.where(row16 == 1, last_low, 0.0)
        ).astype(BF16)
        end_row[g, :, cw:] = jnp.where(row16 == 0, last_high, 0.0).astype(BF16)
        col_high, col_low = split(col)
        row8 = lax.broadcasted_iota(jnp.int32, (8, cw), 0)
        spike[g] = jnp.where(
            row8 < 2, col_high.astype(F32), jnp.where(row8 == 2, col_low.astype(F32), 0.0)
        )
        one = col[:, cw - 1 : cw] if down else col[:, 0:1]
        side, gg = (0, g) if down else (1, g - half)
        for h in range(pieces):
            factor[side, gg * pieces + h : gg * pieces + h + 1, :] = jnp.broadcast_to(one, (1, part))

    sub = lax.broadcasted_iota(jnp.int32, (ns, cw), 0)
    row8b = lax.broadcasted_iota(jnp.int32, (8, rows), 0)

    for it in range(ITERS):
        def moment_step(x, carry):
            sums = list(carry)
            total = None
            for g in range(groups):
                f = cur[pl.ds(pl.multiple_of(g * rows + x * ns, ns), ns), :]
                wf = qw[g, x] * f
                sums[g] = sums[g] + wf
                total = wf if total is None else total + wf
            sums[groups] = sums[groups] + vx[x] * total
            return tuple(sums)

        sums = lax.fori_loop(0, nx, moment_step, (zero,) * (groups + 1), unroll=2)
        density = sums[0]
        along_y = vy[0] * sums[0]
        for g in range(1, groups):
            density = density + sums[g]
            along_y = along_y + vy[g] * sums[g]
        speed_x = sums[groups] / density
        speed_y = along_y / density
        solid_now = solid_part * density

        def equil_step(x, carry):
            diff = vx[x] - speed_x
            e = jnp.exp(-0.5 * (diff * diff))
            ex[x] = e
            tx[x] = solid_now * rx[x] + inlet_part * ix[x]
            return tuple(carry[g] + qw[g, x] * e for g in range(groups))

        sums = lax.fori_loop(0, nx, equil_step, (zero,) * groups, unroll=2)
        zsum = zero
        vertical = []
        for g in range(groups):
            diff = vy[g] - speed_y
            e = jnp.exp(-0.5 * (diff * diff))
            vertical.append(e)
            zsum = zsum + e * sums[g]
        scale = RELAX * density / zsum
        for g in range(groups):
            eya[g] = scale * vertical[g]

        for g in range(groups):
            for copy in halo_copies(it, g):
                copy.wait()

        def rhs_step(x, carry):
            v = vx[x]
            from_left = CFL_STREAM * jnp.maximum(v, 0.0)
            from_right = CFL_STREAM * jnp.maximum(-v, 0.0)
            stay = keep - (from_left + from_right)
            e = ex[x]
            t = tx[x]
            for g in range(groups):
                here = pl.ds(pl.multiple_of(g * rows + x * ns, ns), ns)
                f = cur[here, :]
                low = halo_l[it, pl.ds(g * nx + x, 1), :]
                high = halo_r[it, pl.ds(g * nx + x, 1), :]
                lower = jnp.where(sub == 0, low, pltpu.roll(f, 1, 0))
                upper = jnp.where(sub == ns - 1, high, pltpu.roll(f, ns - 1, 0))
                rhs[here, :] = (
                    stay * f + from_left * lower + from_right * upper + eya[g] * e + ry[g] * t
                )
            return carry

        lax.fori_loop(0, nx, rhs_step, 0, unroll=2)

        def wall_copy(peer, side):
            return pltpu.make_async_remote_copy(
                src_ref=ends.at[it, side], dst_ref=others.at[it, wall],
                send_sem=ws_sem.at[it, peer], recv_sem=wr_sem.at[it, wall],
                device_id=(peer, stream), device_id_type=MESH,
            )

        def wall_arrival(peer):
            return pltpu.make_async_remote_copy(
                src_ref=ends.at[it, 0], dst_ref=others.at[it, peer],
                send_sem=ws_sem.at[it, peer], recv_sem=wr_sem.at[it, peer],
                device_id=(peer, stream), device_id_type=MESH,
            )

        for side in range(2):
            for gg in range(half):
                g = side * half + gg
                here = pl.ds(g * rows, rows)
                high, low = split(rhs[here, :])
                packed[here, 0:cw] = high
                packed[here, cw:] = low
                two = lax.dot_general(
                    end_row[g], packed[here, :], NT, preferred_element_type=F32
                )
                end = two[0:1, :] + two[1:2, :]
                for h in range(pieces):
                    ends[it, side, gg * pieces + h : gg * pieces + h + 1, :] = end[
                        :, h * part : (h + 1) * part
                    ]
            for peer in range(n_wall):
                @pl.when((peer > wall) if side == 0 else (peer < wall))
                def _():
                    wall_copy(peer, side).start()

        for g in range(groups):
            here = pl.ds(g * rows, rows)
            two = lax.dot_general(
                packed[here, :], weight[g], NT, preferred_element_type=F32
            )
            cur[here, :] = two[:, 0:cw] + two[:, cw:]

        before[...] = jnp.zeros_like(before)
        for peer in range(n_wall):
            @pl.when(peer < wall)
            def _():
                wall_arrival(peer).wait_recv()
                before[0] = factor[0] * before[0] + others[it, peer]
        for peer in reversed(range(n_wall)):
            @pl.when(peer > wall)
            def _():
                wall_arrival(peer).wait_recv()
                before[1] = factor[1] * before[1] + others[it, peer]

        for g in range(groups):
            side, gg = (0, g) if g < half else (1, g - half)
            here = pl.ds(g * rows, rows)
            b = jnp.concatenate(
                [before[side, gg * pieces + h : gg * pieces + h + 1, :] for h in range(pieces)],
                axis=1,
            )
            high, low = split(b)
            high = high.astype(F32)
            low = low.astype(F32)
            left_hand = jnp.where(row8b == 1, low, jnp.where(row8b < 3, high, 0.0))
            value = cur[here, :] + lax.dot_general(
                left_hand, spike[g], TN, preferred_element_type=F32
            )
            if it == ITERS - 1:
                out[here, :] = value
            else:
                cur[here, :] = value
                send_edges(it + 1, g)

        for peer in range(n_wall):
            @pl.when(peer != wall)
            def _():
                wall_arrival(peer).wait_send()


def on_device(n_wall, n_stream, dist, quad_weight, vel_x, vel_y, flags, block_inverse, line_coupling):
    groups, nx, ns, cw = dist.shape
    lines = groups * nx
    total = lines * ns
    rows = nx * ns
    pieces = 8 // (groups // 2)
    part = rows // pieces
    flat = dist.reshape(total, cw)
    smem = pl.BlockSpec(memory_space=pltpu.SMEM)
    vmem = pl.BlockSpec(memory_space=pltpu.VMEM)
    result = pl.pallas_call(
        functools.partial(kernel, groups, nx, ns, n_wall, n_stream),
        out_shape=jax.ShapeDtypeStruct((total, cw), F32),
        in_specs=[pl.BlockSpec(memory_space=pl.ANY), smem, smem, smem, vmem, vmem, smem],
        out_specs=vmem,
        scratch_shapes=[
            pltpu.VMEM((total, cw), F32),
            pltpu.VMEM((total, cw), F32),
            pltpu.VMEM((total, 2 * cw), BF16),
            pltpu.VMEM((groups, 2 * cw, 2 * cw), BF16),
            pltpu.VMEM((groups, 16, 2 * cw), BF16),
            pltpu.VMEM((groups, 8, cw), F32),
            pltpu.VMEM((2, 8, part), F32),
            pltpu.VMEM((nx, ns, cw), F32),
            pltpu.VMEM((nx, ns, cw), F32),
            pltpu.VMEM((nx, ns, cw), F32),
            pltpu.VMEM((nx, ns, cw), F32),
            pltpu.VMEM((groups, ns, cw), F32),
            pltpu.VMEM((groups, ns, cw), F32),
            pltpu.VMEM((ITERS, lines, cw), F32),
            pltpu.VMEM((ITERS, lines, cw), F32),
            pltpu.VMEM((ITERS, lines, cw), F32),
            pltpu.VMEM((ITERS, lines, cw), F32),
            pltpu.VMEM((ITERS, 2, 8, part), F32),
            pltpu.VMEM((ITERS, n_wall, 8, part), F32),
            pltpu.VMEM((2, 8, part), F32),
            pltpu.SemaphoreType.DMA((groups,)),
            pltpu.SemaphoreType.DMA((ITERS, groups)),
            pltpu.SemaphoreType.DMA((ITERS, groups)),
            pltpu.SemaphoreType.DMA((ITERS, groups)),
            pltpu.SemaphoreType.DMA((ITERS, groups)),
            pltpu.SemaphoreType.DMA((ITERS, n_wall)),
            pltpu.SemaphoreType.DMA((ITERS, n_wall)),
        ],
        compiler_params=pltpu.CompilerParams(
            collective_id=0, has_side_effects=True, vmem_limit_bytes=40 * 1024 * 1024
        ),
    )(flat, quad_weight, vel_x, vel_y, flags, block_inverse, line_coupling)
    return result.reshape(groups, nx, ns, cw)


def solution(mesh):
    return jax.shard_map(
        functools.partial(on_device, mesh.shape["wall"], mesh.shape["stream"]),
        mesh=mesh,
        in_specs=(P(None, None, "stream", "wall"), P(), P(), P(), P("stream", "wall"), P(), P()),
        out_specs=P(None, None, "stream", "wall"),
        check_vma=False,
    )
```

```python
import functools
import jax
import jax.numpy as jnp
from jax import lax
from jax.experimental import pallas as pl
from jax.experimental.pallas import tpu as pltpu
from jax.sharding import PartitionSpec as P

ITERS = 2
CFL_STREAM = 0.12
RELAX = 0.3
PENALTY = 0.5
INLET_SPEED = 0.5
MESH = pl.DeviceIdType.MESH
F32 = jnp.float32
BF16 = jnp.bfloat16
NT = (((1,), (1,)), ((), ()))
TN = (((0,), (0,)), ((), ()))


def split(value):
    high = value.astype(BF16)
    return high, (value - high.astype(F32)).astype(BF16)


def kernel(
    groups, nx, ns, n_wall, n_stream,
    dist, qw_in, vx_in, vy_in, flags_in, inv_in, lc_in,
    out,
    qw, vx, vy, lc, flags, inv, sel, near,
    cur, rhs, packed, weight, end_row, spike, factor, ex, tx, rx, ix, ry, eya,
    edge_l, edge_r, halo_l, halo_r, ends, others, before,
    table_sem, store_sem, ns_sem, nr_sem, load_sem, sl_sem, sr_sem, rl_sem, rr_sem, ws_sem, wr_sem,
):
    cw = cur.shape[1]
    half = groups // 2
    rows = nx * ns
    part = ends.shape[3]
    pieces = rows // part
    wall = lax.axis_index("wall")
    stream = lax.axis_index("stream")
    left = lax.rem(stream + n_stream - 1, n_stream)
    right = lax.rem(stream + 1, n_stream)

    loads = [
        pltpu.make_async_copy(
            dist.at[pl.ds(g * rows, rows)], cur.at[pl.ds(g * rows, rows)], load_sem.at[g]
        )
        for g in range(groups)
    ]
    for load in loads:
        load.start()
    tables = [
        pltpu.make_async_copy(source, target, table_sem.at[i])
        for i, (source, target) in enumerate(
            ((qw_in, qw), (vx_in, vx), (vy_in, vy), (lc_in, lc), (flags_in, flags), (inv_in, inv))
        )
    ]
    for table in tables:
        table.start()

    barrier = pltpu.get_barrier_semaphore()
    for to in (left, right):
        pl.semaphore_signal(barrier, inc=1, device_id=(wall, to), device_id_type=MESH)
    for step in range(1, n_wall):
        to = lax.rem(wall + step, n_wall)
        pl.semaphore_signal(barrier, inc=1, device_id=(to, stream), device_id_type=MESH)
    pl.semaphore_wait(barrier, 2 + n_wall - 1)

    stores = [
        pltpu.make_async_copy(
            cur.at[pl.ds(g * rows, rows)], out.at[pl.ds(g * rows, rows)], store_sem.at[g]
        )
        for g in range(groups)
    ]

    def halo_copies(it, g):
        here = pl.ds(g * nx, nx)
        return (
            pltpu.make_async_remote_copy(
                src_ref=edge_r.at[it, here], dst_ref=halo_l.at[it, here],
                send_sem=sr_sem.at[it, g], recv_sem=rl_sem.at[it, g],
                device_id=(wall, right), device_id_type=MESH,
            ),
            pltpu.make_async_remote_copy(
                src_ref=edge_l.at[it, here], dst_ref=halo_r.at[it, here],
                send_sem=sl_sem.at[it, g], recv_sem=rr_sem.at[it, g],
                device_id=(wall, left), device_id_type=MESH,
            ),
        )

    def send_edges(it, g):
        here = pl.ds(g * nx, nx)
        edge_r[it, here, :] = cur[pl.ds(g * rows + ns - 1, nx, stride=ns), :]
        edge_l[it, here, :] = cur[pl.ds(g * rows, nx, stride=ns), :]
        for copy in halo_copies(it, g):
            copy.start()

    for g in range(groups):
        loads[g].wait()
        send_edges(0, g)

    for table in tables:
        table.wait()
    zero = jnp.zeros((ns, cw), F32)

    def table_step(x, carry):
        v = jnp.full((ns, cw), vx[x], F32)
        rest = jnp.exp(-0.5 * (v * v))
        shifted = v - INLET_SPEED
        inlet = jnp.exp(-0.5 * (shifted * shifted))
        rx[x] = rest
        ix[x] = inlet
        sums = list(carry)
        for g in range(groups):
            w = qw[g, x]
            sums[g] = sums[g] + w * rest
            sums[groups + g] = sums[groups + g] + w * inlet
        return tuple(sums)

    sums = lax.fori_loop(0, nx, table_step, (zero,) * (2 * groups))
    rest_sum = zero
    inlet_sum = zero
    for g in range(groups):
        v = jnp.full((ns, cw), vy[g], F32)
        factor_y = jnp.exp(-0.5 * (v * v))
        ry[g] = factor_y
        rest_sum = rest_sum + factor_y * sums[g]
        inlet_sum = inlet_sum + factor_y * sums[groups + g]
    kind = flags[...]
    solid = jnp.where(kind == 1, PENALTY, 0.0).astype(F32)
    inflow = jnp.where(kind == 2, PENALTY, 0.0).astype(F32)
    keep = 1.0 - solid - inflow
    solid_part = solid / rest_sum
    inlet_part = inflow / inlet_sum

    row16 = lax.broadcasted_iota(jnp.int32, (16, cw), 0)
    for g in range(groups):
        m = inv[g]
        high, low = split(m)
        weight[g, 0:cw, 0:cw] = high
        weight[g, 0:cw, cw:] = high
        weight[g, cw:, 0:cw] = low
        weight[g, cw:, cw:] = jnp.zeros((cw, cw), BF16)
        mt = m.T
        down = g < half
        last = m[cw - 1 : cw, :] if down else m[0:1, :]
        col = (mt[0:1, :] if down else mt[cw - 1 : cw, :]) * lc[g]
        last_high, last_low = split(last)
        last_high = last_high.astype(F32)
        last_low = last_low.astype(F32)
        end_row[g, :, 0:cw] = jnp.where(
            row16 == 0, last_high, jnp.where(row16 == 1, last_low, 0.0)
        ).astype(BF16)
        end_row[g, :, cw:] = jnp.where(row16 == 0, last_high, 0.0).astype(BF16)
        col_high, col_low = split(col)
        row8 = lax.broadcasted_iota(jnp.int32, (8, cw), 0)
        spike[g] = jnp.where(
            row8 < 2, col_high.astype(F32), jnp.where(row8 == 2, col_low.astype(F32), 0.0)
        )
        one = col[:, cw - 1 : cw] if down else col[:, 0:1]
        side, gg = (0, g) if down else (1, g - half)
        for h in range(pieces):
            factor[side, gg * pieces + h : gg * pieces + h + 1, :] = jnp.broadcast_to(one, (1, part))

    lane = lax.broadcasted_iota(jnp.int32, (part, nx), 0)
    line = lax.broadcasted_iota(jnp.int32, (part, nx), 1)
    for way, node in enumerate((ns - 1, 0)):
        for h in range(pieces):
            wanted = (line * ns + node) == (lane + h * part)
            sel[way, h] = jnp.where(wanted, 1.0, 0.0).astype(BF16)
    row8n = lax.broadcasted_iota(jnp.int32, (8, nx), 0)

    def near_copies():
        return [
            pltpu.make_async_remote_copy(
                src_ref=before, dst_ref=near.at[way],
                send_sem=ns_sem.at[way], recv_sem=nr_sem.at[way],
                device_id=(wall, to), device_id_type=MESH,
            )
            for way, to in enumerate((right, left))
        ]

    sub = lax.broadcasted_iota(jnp.int32, (ns, cw), 0)
    row8b = lax.broadcasted_iota(jnp.int32, (8, rows), 0)

    for it in range(ITERS):
        def moment_step(x, carry):
            sums = list(carry)
            total = None
            for g in range(groups):
                f = cur[pl.ds(pl.multiple_of(g * rows + x * ns, ns), ns), :]
                wf = qw[g, x] * f
                sums[g] = sums[g] + wf
                total = wf if total is None else total + wf
            sums[groups] = sums[groups] + vx[x] * total
            return tuple(sums)

        sums = lax.fori_loop(0, nx, moment_step, (zero,) * (groups + 1), unroll=2)
        density = sums[0]
        along_y = vy[0] * sums[0]
        for g in range(1, groups):
            density = density + sums[g]
            along_y = along_y + vy[g] * sums[g]
        speed_x = sums[groups] / density
        speed_y = along_y / density
        solid_now = solid_part * density

        def equil_step(x, carry):
            diff = vx[x] - speed_x
            e = jnp.exp(-0.5 * (diff * diff))
            ex[x] = e
            tx[x] = solid_now * rx[x] + inlet_part * ix[x]
            return tuple(carry[g] + qw[g, x] * e for g in range(groups))

        sums = lax.fori_loop(0, nx, equil_step, (zero,) * groups, unroll=2)
        zsum = zero
        vertical = []
        for g in range(groups):
            diff = vy[g] - speed_y
            e = jnp.exp(-0.5 * (diff * diff))
            vertical.append(e)
            zsum = zsum + e * sums[g]
        scale = RELAX * density / zsum
        for g in range(groups):
            eya[g] = scale * vertical[g]

        for g in range(groups):
            for copy in halo_copies(it, g):
                copy.wait()
        if it > 0:
            for copy in near_copies():
                copy.wait()
            for way, halo in enumerate((halo_l, halo_r)):
                picked = []
                both = near[way].reshape(16, part)
                high, low = split(both)
                for h in range(pieces):
                    picked.append((
                        jnp.dot(high, sel[way, h], preferred_element_type=F32),
                        jnp.dot(low, sel[way, h], preferred_element_type=F32),
                    ))
                for g in range(groups):
                    high = low = None
                    for h in range(pieces):
                        r = g * pieces + h
                        p_high = picked[h][0][r : r + 1, :]
                        p_low = picked[h][1][r : r + 1, :]
                        high = p_high if high is None else high + p_high
                        low = p_low if low is None else low + p_low
                    left_hand = jnp.where(row8n == 1, low, jnp.where(row8n < 3, high, 0.0))
                    here = pl.ds(g * nx, nx)
                    halo[it, here, :] = halo[it, here, :] + lax.dot_general(
                        left_hand, spike[g], TN, preferred_element_type=F32
                    )

        def rhs_step(x, carry):
            v = vx[x]
            from_left = CFL_STREAM * jnp.maximum(v, 0.0)
            from_right = CFL_STREAM * jnp.maximum(-v, 0.0)
            stay = keep - (from_left + from_right)
            e = ex[x]
            t = tx[x]
            for g in range(groups):
                here = pl.ds(pl.multiple_of(g * rows + x * ns, ns), ns)
                f = cur[here, :]
                low = halo_l[it, pl.ds(g * nx + x, 1), :]
                high = halo_r[it, pl.ds(g * nx + x, 1), :]
                lower = jnp.where(sub == 0, low, pltpu.roll(f, 1, 0))
                upper = jnp.where(sub == ns - 1, high, pltpu.roll(f, ns - 1, 0))
                rhs[here, :] = (
                    stay * f + from_left * lower + from_right * upper + eya[g] * e + ry[g] * t
                )
            return carry

        lax.fori_loop(0, nx, rhs_step, 0, unroll=2)

        def wall_copy(peer, side):
            return pltpu.make_async_remote_copy(
                src_ref=ends.at[it, side], dst_ref=others.at[it, wall],
                send_sem=ws_sem.at[it, peer], recv_sem=wr_sem.at[it, wall],
                device_id=(peer, stream), device_id_type=MESH,
            )

        def wall_arrival(peer):
            return pltpu.make_async_remote_copy(
                src_ref=ends.at[it, 0], dst_ref=others.at[it, peer],
                send_sem=ws_sem.at[it, peer], recv_sem=wr_sem.at[it, peer],
                device_id=(peer, stream), device_id_type=MESH,
            )

        for side in range(2):
            for gg in range(half):
                g = side * half + gg
                here = pl.ds(g * rows, rows)
                high, low = split(rhs[here, :])
                packed[here, 0:cw] = high
                packed[here, cw:] = low
                two = lax.dot_general(
                    end_row[g], packed[here, :], NT, preferred_element_type=F32
                )
                end = two[0:1, :] + two[1:2, :]
                for h in range(pieces):
                    ends[it, side, gg * pieces + h : gg * pieces + h + 1, :] = end[
                        :, h * part : (h + 1) * part
                    ]
            for peer in range(n_wall):
                @pl.when((peer > wall) if side == 0 else (peer < wall))
                def _():
                    wall_copy(peer, side).start()

        for g in range(groups):
            here = pl.ds(g * rows, rows)
            two = lax.dot_general(
                packed[here, :], weight[g], NT, preferred_element_type=F32
            )
            cur[here, :] = two[:, 0:cw] + two[:, cw:]
            if it < ITERS - 1:
                send_edges(it + 1, g)

        before[...] = jnp.zeros_like(before)
        for peer in range(n_wall):
            @pl.when(peer < wall)
            def _():
                wall_arrival(peer).wait_recv()
                before[0] = factor[0] * before[0] + others[it, peer]
        for peer in reversed(range(n_wall)):
            @pl.when(peer > wall)
            def _():
                wall_arrival(peer).wait_recv()
                before[1] = factor[1] * before[1] + others[it, peer]

        if it < ITERS - 1:
            for copy in near_copies():
                copy.start()
        for g in range(groups):
            side, gg = (0, g) if g < half else (1, g - half)
            here = pl.ds(g * rows, rows)
            b = jnp.concatenate(
                [before[side, gg * pieces + h : gg * pieces + h + 1, :] for h in range(pieces)],
                axis=1,
            )
            high, low = split(b)
            high = high.astype(F32)
            low = low.astype(F32)
            left_hand = jnp.where(row8b == 1, low, jnp.where(row8b < 3, high, 0.0))
            value = cur[here, :] + lax.dot_general(
                left_hand, spike[g], TN, preferred_element_type=F32
            )
            cur[here, :] = value
            if it == ITERS - 1:
                stores[g].start()

        for peer in range(n_wall):
            @pl.when(peer != wall)
            def _():
                wall_arrival(peer).wait_send()
    for store in stores:
        store.wait()


def on_device(n_wall, n_stream, dist, quad_weight, vel_x, vel_y, flags, block_inverse, line_coupling):
    groups, nx, ns, cw = dist.shape
    lines = groups * nx
    total = lines * ns
    rows = nx * ns
    pieces = 8 // (groups // 2)
    part = rows // pieces
    flat = dist.reshape(total, cw)
    anywhere = pl.BlockSpec(memory_space=pl.ANY)
    result = pl.pallas_call(
        functools.partial(kernel, groups, nx, ns, n_wall, n_stream),
        out_shape=jax.ShapeDtypeStruct((total, cw), F32),
        in_specs=[anywhere] * 7,
        out_specs=anywhere,
        scratch_shapes=[
            pltpu.SMEM((groups, nx), F32),
            pltpu.SMEM((nx,), F32),
            pltpu.SMEM((groups,), F32),
            pltpu.SMEM((groups,), F32),
            pltpu.VMEM((ns, cw), jnp.int32),
            pltpu.VMEM((groups, cw, cw), F32),
            pltpu.VMEM((2, pieces, part, nx), BF16),
            pltpu.VMEM((2, 2, 8, part), F32),
            pltpu.VMEM((total, cw), F32),
            pltpu.VMEM((total, cw), F32),
            pltpu.VMEM((total, 2 * cw), BF16),
            pltpu.VMEM((groups, 2 * cw, 2 * cw), BF16),
            pltpu.VMEM((groups, 16, 2 * cw), BF16),
            pltpu.VMEM((groups, 8, cw), F32),
            pltpu.VMEM((2, 8, part), F32),
            pltpu.VMEM((nx, ns, cw), F32),
            pltpu.VMEM((nx, ns, cw), F32),
            pltpu.VMEM((nx, ns, cw), F32),
            pltpu.VMEM((nx, ns, cw), F32),
            pltpu.VMEM((groups, ns, cw), F32),
            pltpu.VMEM((groups, ns, cw), F32),
            pltpu.VMEM((ITERS, lines, cw), F32),
            pltpu.VMEM((ITERS, lines, cw), F32),
            pltpu.VMEM((ITERS, lines, cw), F32),
            pltpu.VMEM((ITERS, lines, cw), F32),
            pltpu.VMEM((ITERS, 2, 8, part), F32),
            pltpu.VMEM((ITERS, n_wall, 8, part), F32),
            pltpu.VMEM((2, 8, part), F32),
            pltpu.SemaphoreType.DMA((6,)),
            pltpu.SemaphoreType.DMA((groups,)),
            pltpu.SemaphoreType.DMA((2,)),
            pltpu.SemaphoreType.DMA((2,)),
            pltpu.SemaphoreType.DMA((groups,)),
            pltpu.SemaphoreType.DMA((ITERS, groups)),
            pltpu.SemaphoreType.DMA((ITERS, groups)),
            pltpu.SemaphoreType.DMA((ITERS, groups)),
            pltpu.SemaphoreType.DMA((ITERS, groups)),
            pltpu.SemaphoreType.DMA((ITERS, n_wall)),
            pltpu.SemaphoreType.DMA((ITERS, n_wall)),
        ],
        compiler_params=pltpu.CompilerParams(
            collective_id=0, has_side_effects=True, vmem_limit_bytes=63 * 1024 * 1024
        ),
    )(flat, quad_weight, vel_x, vel_y, flags, block_inverse, line_coupling)
    return result.reshape(groups, nx, ns, cw)


def solution(mesh):
    return jax.shard_map(
        functools.partial(on_device, mesh.shape["wall"], mesh.shape["stream"]),
        mesh=mesh,
        in_specs=(P(None, None, "stream", "wall"), P(), P(), P(), P("stream", "wall"), P(), P()),
        out_specs=P(None, None, "stream", "wall"),
        check_vma=False,
    )
```

```python
import functools
import jax
import jax.numpy as jnp
from jax import lax
from jax.experimental import pallas as pl
from jax.experimental.pallas import tpu as pltpu
from jax.sharding import PartitionSpec as P

ITERS = 2
CFL_STREAM = 0.12
RELAX = 0.3
PENALTY = 0.5
INLET_SPEED = 0.5
MESH = pl.DeviceIdType.MESH
F32 = jnp.float32
BF16 = jnp.bfloat16
NT = (((1,), (1,)), ((), ()))
TN = (((0,), (0,)), ((), ()))


def split(value):
    high = value.astype(BF16)
    return high, (value - high.astype(F32)).astype(BF16)


def kernel(
    groups, nx, ns, n_wall, n_stream,
    dist, qw_in, vx_in, vy_in, flags_in, inv_in, lc_in,
    out,
    qw, vx, vy, lc, flags, inv, sel, near, pull_l, pull_r,
    cur, rhs, packed, weight, end_row, spike, factor, ex, tx, rx, ix, ry, eya,
    edge_l, edge_r, halo_l, halo_r, ends, others, before,
    table_sem, ns_sem, nr_sem, load_sem, sl_sem, sr_sem, rl_sem, rr_sem, ws_sem, wr_sem,
):
    cw = cur.shape[1]
    half = groups // 2
    rows = nx * ns
    part = ends.shape[3]
    pieces = rows // part
    wall = lax.axis_index("wall")
    stream = lax.axis_index("stream")
    left = lax.rem(stream + n_stream - 1, n_stream)
    right = lax.rem(stream + 1, n_stream)

    loads = [
        pltpu.make_async_copy(
            dist.at[pl.ds(g * rows, rows)], cur.at[pl.ds(g * rows, rows)], load_sem.at[g]
        )
        for g in range(groups)
    ]
    for load in loads:
        load.start()
    tables = [
        pltpu.make_async_copy(source, target, table_sem.at[i])
        for i, (source, target) in enumerate(
            ((qw_in, qw), (vx_in, vx), (vy_in, vy), (lc_in, lc), (flags_in, flags), (inv_in, inv))
        )
    ]
    for table in tables:
        table.start()

    barrier = pltpu.get_barrier_semaphore()
    for to in (left, right):
        pl.semaphore_signal(barrier, inc=1, device_id=(wall, to), device_id_type=MESH)
    for step in range(1, n_wall):
        to = lax.rem(wall + step, n_wall)
        pl.semaphore_signal(barrier, inc=1, device_id=(to, stream), device_id_type=MESH)
    pl.semaphore_wait(barrier, 2 + n_wall - 1)

    def halo_copies(it, g):
        here = pl.ds(g * nx, nx)
        return (
            pltpu.make_async_remote_copy(
                src_ref=edge_r.at[it, here], dst_ref=halo_l.at[it, here],
                send_sem=sr_sem.at[it, g], recv_sem=rl_sem.at[it, g],
                device_id=(wall, right), device_id_type=MESH,
            ),
            pltpu.make_async_remote_copy(
                src_ref=edge_l.at[it, here], dst_ref=halo_r.at[it, here],
                send_sem=sl_sem.at[it, g], recv_sem=rr_sem.at[it, g],
                device_id=(wall, left), device_id_type=MESH,
            ),
        )

    def send_edges(it, g):
        here = pl.ds(g * nx, nx)
        edge_r[it, here, :] = cur[pl.ds(g * rows + ns - 1, nx, stride=ns), :]
        edge_l[it, here, :] = cur[pl.ds(g * rows, nx, stride=ns), :]
        for copy in halo_copies(it, g):
            copy.start()

    for g in range(groups):
        loads[g].wait()
        send_edges(0, g)

    for table in tables:
        table.wait()
    zero = jnp.zeros((ns, cw), F32)

    def table_step(x, carry):
        v = jnp.full((ns, cw), vx[x], F32)
        rest = jnp.exp(-0.5 * (v * v))
        shifted = v - INLET_SPEED
        inlet = jnp.exp(-0.5 * (shifted * shifted))
        pull_l[pl.ds(x, 1), :] = CFL_STREAM * jnp.maximum(v[0:1, :], 0.0)
        pull_r[pl.ds(x, 1), :] = CFL_STREAM * jnp.maximum(-v[0:1, :], 0.0)
        rx[x] = rest
        ix[x] = inlet
        sums = list(carry)
        for g in range(groups):
            w = qw[g, x]
            sums[g] = sums[g] + w * rest
            sums[groups + g] = sums[groups + g] + w * inlet
        return tuple(sums)

    sums = lax.fori_loop(0, nx, table_step, (zero,) * (2 * groups), unroll=4)
    rest_sum = zero
    inlet_sum = zero
    for g in range(groups):
        v = jnp.full((ns, cw), vy[g], F32)
        factor_y = jnp.exp(-0.5 * (v * v))
        ry[g] = factor_y
        rest_sum = rest_sum + factor_y * sums[g]
        inlet_sum = inlet_sum + factor_y * sums[groups + g]
    kind = flags[...]
    solid = jnp.where(kind == 1, PENALTY, 0.0).astype(F32)
    inflow = jnp.where(kind == 2, PENALTY, 0.0).astype(F32)
    keep = 1.0 - solid - inflow
    solid_part = solid / rest_sum
    inlet_part = inflow / inlet_sum

    row16 = lax.broadcasted_iota(jnp.int32, (16, cw), 0)
    for g in range(groups):
        m = inv[g]
        high, low = split(m)
        weight[g, 0:cw, 0:cw] = high
        weight[g, 0:cw, cw:] = high
        weight[g, cw:, 0:cw] = low
        weight[g, cw:, cw:] = jnp.zeros((cw, cw), BF16)
        mt = m.T
        down = g < half
        last = m[cw - 1 : cw, :] if down else m[0:1, :]
        col = (mt[0:1, :] if down else mt[cw - 1 : cw, :]) * lc[g]
        last_high, last_low = split(last)
        last_high = last_high.astype(F32)
        last_low = last_low.astype(F32)
        end_row[g, :, 0:cw] = jnp.where(
            row16 == 0, last_high, jnp.where(row16 == 1, last_low, 0.0)
        ).astype(BF16)
        end_row[g, :, cw:] = jnp.where(row16 == 0, last_high, 0.0).astype(BF16)
        col_high, col_low = split(col)
        row8 = lax.broadcasted_iota(jnp.int32, (8, cw), 0)
        spike[g] = jnp.where(
            row8 < 2, col_high.astype(F32), jnp.where(row8 == 2, col_low.astype(F32), 0.0)
        )
        one = col[:, cw - 1 : cw] if down else col[:, 0:1]
        side, gg = (0, g) if down else (1, g - half)
        for h in range(pieces):
            factor[side, gg * pieces + h : gg * pieces + h + 1, :] = jnp.broadcast_to(one, (1, part))

    lane = lax.broadcasted_iota(jnp.int32, (part, nx), 0)
    line = lax.broadcasted_iota(jnp.int32, (part, nx), 1)
    for way, node in enumerate((ns - 1, 0)):
        for h in range(pieces):
            wanted = (line * ns + node) == (lane + h * part)
            sel[way, h] = jnp.where(wanted, 1.0, 0.0).astype(BF16)
    row8n = lax.broadcasted_iota(jnp.int32, (8, nx), 0)

    def near_copies():
        return [
            pltpu.make_async_remote_copy(
                src_ref=before, dst_ref=near.at[way],
                send_sem=ns_sem.at[way], recv_sem=nr_sem.at[way],
                device_id=(wall, to), device_id_type=MESH,
            )
            for way, to in enumerate((right, left))
        ]

    sub = lax.broadcasted_iota(jnp.int32, (ns, cw), 0)
    row8b = lax.broadcasted_iota(jnp.int32, (8, rows), 0)

    for it in range(ITERS):
        def moment_step(x, carry):
            sums = list(carry)
            total = None
            for g in range(groups):
                f = cur[pl.ds(pl.multiple_of(g * rows + x * ns, ns), ns), :]
                wf = qw[g, x] * f
                sums[g] = sums[g] + wf
                total = wf if total is None else total + wf
            sums[groups] = sums[groups] + vx[x] * total
            return tuple(sums)

        sums = lax.fori_loop(0, nx, moment_step, (zero,) * (groups + 1), unroll=4)
        density = sums[0]
        along_y = vy[0] * sums[0]
        for g in range(1, groups):
            density = density + sums[g]
            along_y = along_y + vy[g] * sums[g]
        speed_x = sums[groups] / density
        speed_y = along_y / density
        solid_now = solid_part * density

        def equil_step(x, carry):
            diff = vx[x] - speed_x
            e = jnp.exp(-0.5 * (diff * diff))
            ex[x] = e
            tx[x] = solid_now * rx[x] + inlet_part * ix[x]
            return tuple(carry[g] + qw[g, x] * e for g in range(groups))

        sums = lax.fori_loop(0, nx, equil_step, (zero,) * groups, unroll=4)
        zsum = zero
        vertical = []
        for g in range(groups):
            diff = vy[g] - speed_y
            e = jnp.exp(-0.5 * (diff * diff))
            vertical.append(e)
            zsum = zsum + e * sums[g]
        scale = RELAX * density / zsum
        for g in range(groups):
            eya[g] = scale * vertical[g]

        def rhs_step(x, carry):
            v = vx[x]
            from_left = CFL_STREAM * jnp.maximum(v, 0.0)
            from_right = CFL_STREAM * jnp.maximum(-v, 0.0)
            stay = keep - (from_left + from_right)
            inner_left = jnp.where(sub == 0, 0.0, from_left)
            inner_right = jnp.where(sub == ns - 1, 0.0, from_right)
            e = ex[x]
            t = tx[x]
            for g in range(groups):
                here = pl.ds(pl.multiple_of(g * rows + x * ns, ns), ns)
                f = cur[here, :]
                rhs[here, :] = (
                    stay * f
                    + inner_left * pltpu.roll(f, 1, 0)
                    + inner_right * pltpu.roll(f, ns - 1, 0)
                    + eya[g] * e
                    + ry[g] * t
                )
            return carry

        lax.fori_loop(0, nx, rhs_step, 0, unroll=4)

        def wall_copy(peer, side):
            return pltpu.make_async_remote_copy(
                src_ref=ends.at[it, side], dst_ref=others.at[it, wall],
                send_sem=ws_sem.at[it, peer], recv_sem=wr_sem.at[it, wall],
                device_id=(peer, stream), device_id_type=MESH,
            )

        def wall_arrival(peer):
            return pltpu.make_async_remote_copy(
                src_ref=ends.at[it, 0], dst_ref=others.at[it, peer],
                send_sem=ws_sem.at[it, peer], recv_sem=wr_sem.at[it, peer],
                device_id=(peer, stream), device_id_type=MESH,
            )

        picks = []
        if it > 0:
            for copy in near_copies():
                copy.wait()
            for way in range(2):
                high, low = split(near[way].reshape(16, part))
                picks.append([
                    (
                        jnp.dot(high, sel[way, h], preferred_element_type=F32),
                        jnp.dot(low, sel[way, h], preferred_element_type=F32),
                    )
                    for h in range(pieces)
                ])

        def add_halo(g):
            for copy in halo_copies(it, g):
                copy.wait()
            for way, (halo, pull) in enumerate(((halo_l, pull_l), (halo_r, pull_r))):
                value = halo[it, pl.ds(g * nx, nx), :]
                if it > 0:
                    high = low = None
                    for h in range(pieces):
                        r = g * pieces + h
                        p_high = picks[way][h][0][r : r + 1, :]
                        p_low = picks[way][h][1][r : r + 1, :]
                        high = p_high if high is None else high + p_high
                        low = p_low if low is None else low + p_low
                    left_hand = jnp.where(row8n == 1, low, jnp.where(row8n < 3, high, 0.0))
                    value = value + lax.dot_general(
                        left_hand, spike[g], TN, preferred_element_type=F32
                    )
                edge = pl.ds(g * rows + (0 if way == 0 else ns - 1), nx, stride=ns)
                rhs[edge, :] = rhs[edge, :] + pull[...] * value

        for side in range(2):
            for gg in range(half):
                g = side * half + gg
                here = pl.ds(g * rows, rows)
                add_halo(g)
                high, low = split(rhs[here, :])
                packed[here, 0:cw] = high
                packed[here, cw:] = low
                two = lax.dot_general(
                    end_row[g], packed[here, :], NT, preferred_element_type=F32
                )
                end = two[0:1, :] + two[1:2, :]
                for h in range(pieces):
                    ends[it, side, gg * pieces + h : gg * pieces + h + 1, :] = end[
                        :, h * part : (h + 1) * part
                    ]
            for peer in range(n_wall):
                @pl.when((peer > wall) if side == 0 else (peer < wall))
                def _():
                    wall_copy(peer, side).start()

        for g in range(groups):
            here = pl.ds(g * rows, rows)
            two = lax.dot_general(
                packed[here, :], weight[g], NT, preferred_element_type=F32
            )
            cur[here, :] = two[:, 0:cw] + two[:, cw:]
            if it < ITERS - 1:
                send_edges(it + 1, g)

        before[...] = jnp.zeros_like(before)
        for peer in range(n_wall):
            @pl.when(peer < wall)
            def _():
                wall_arrival(peer).wait_recv()
                before[0] = factor[0] * before[0] + others[it, peer]
        for peer in reversed(range(n_wall)):
            @pl.when(peer > wall)
            def _():
                wall_arrival(peer).wait_recv()
                before[1] = factor[1] * before[1] + others[it, peer]

        if it < ITERS - 1:
            for copy in near_copies():
                copy.start()
        for g in range(groups):
            side, gg = (0, g) if g < half else (1, g - half)
            here = pl.ds(g * rows, rows)
            b = jnp.concatenate(
                [before[side, gg * pieces + h : gg * pieces + h + 1, :] for h in range(pieces)],
                axis=1,
            )
            high, low = split(b)
            high = high.astype(F32)
            low = low.astype(F32)
            left_hand = jnp.where(row8b == 1, low, jnp.where(row8b < 3, high, 0.0))
            value = cur[here, :] + lax.dot_general(
                left_hand, spike[g], TN, preferred_element_type=F32
            )
            if it == ITERS - 1:
                out[here, :] = value
            else:
                cur[here, :] = value

        for peer in range(n_wall):
            @pl.when(peer != wall)
            def _():
                wall_arrival(peer).wait_send()


def on_device(n_wall, n_stream, dist, quad_weight, vel_x, vel_y, flags, block_inverse, line_coupling):
    groups, nx, ns, cw = dist.shape
    lines = groups * nx
    total = lines * ns
    rows = nx * ns
    pieces = 8 // (groups // 2)
    part = rows // pieces
    flat = dist.reshape(total, cw)
    hbm = pl.BlockSpec(memory_space=pltpu.HBM)
    vmem = pl.BlockSpec(memory_space=pltpu.VMEM)
    result = pl.pallas_call(
        functools.partial(kernel, groups, nx, ns, n_wall, n_stream),
        out_shape=pltpu.VMEM((total, cw), F32),
        in_specs=[hbm] * 7,
        out_specs=vmem,
        scratch_shapes=[
            pltpu.SMEM((groups, nx), F32),
            pltpu.SMEM((nx,), F32),
            pltpu.SMEM((groups,), F32),
            pltpu.SMEM((groups,), F32),
            pltpu.VMEM((ns, cw), jnp.int32),
            pltpu.VMEM((groups, cw, cw), F32),
            pltpu.VMEM((2, pieces, part, nx), BF16),
            pltpu.VMEM((2, 2, 8, part), F32),
            pltpu.VMEM((nx, cw), F32),
            pltpu.VMEM((nx, cw), F32),
            pltpu.VMEM((total, cw), F32),
            pltpu.VMEM((total, cw), F32),
            pltpu.VMEM((total, 2 * cw), BF16),
            pltpu.VMEM((groups, 2 * cw, 2 * cw), BF16),
            pltpu.VMEM((groups, 16, 2 * cw), BF16),
            pltpu.VMEM((groups, 8, cw), F32),
            pltpu.VMEM((2, 8, part), F32),
            pltpu.VMEM((nx, ns, cw), F32),
            pltpu.VMEM((nx, ns, cw), F32),
            pltpu.VMEM((nx, ns, cw), F32),
            pltpu.VMEM((nx, ns, cw), F32),
            pltpu.VMEM((groups, ns, cw), F32),
            pltpu.VMEM((groups, ns, cw), F32),
            pltpu.VMEM((ITERS, lines, cw), F32),
            pltpu.VMEM((ITERS, lines, cw), F32),
            pltpu.VMEM((ITERS, lines, cw), F32),
            pltpu.VMEM((ITERS, lines, cw), F32),
            pltpu.VMEM((ITERS, 2, 8, part), F32),
            pltpu.VMEM((ITERS, n_wall, 8, part), F32),
            pltpu.VMEM((2, 8, part), F32),
            pltpu.SemaphoreType.DMA((6,)),
            pltpu.SemaphoreType.DMA((2,)),
            pltpu.SemaphoreType.DMA((2,)),
            pltpu.SemaphoreType.DMA((groups,)),
            pltpu.SemaphoreType.DMA((ITERS, groups)),
            pltpu.SemaphoreType.DMA((ITERS, groups)),
            pltpu.SemaphoreType.DMA((ITERS, groups)),
            pltpu.SemaphoreType.DMA((ITERS, groups)),
            pltpu.SemaphoreType.DMA((ITERS, n_wall)),
            pltpu.SemaphoreType.DMA((ITERS, n_wall)),
        ],
        compiler_params=pltpu.CompilerParams(
            collective_id=0, has_side_effects=True, vmem_limit_bytes=52 * 1024 * 1024
        ),
    )(flat, quad_weight, vel_x, vel_y, flags, block_inverse, line_coupling)
    return result.reshape(groups, nx, ns, cw)


def solution(mesh):
    return jax.shard_map(
        functools.partial(on_device, mesh.shape["wall"], mesh.shape["stream"]),
        mesh=mesh,
        in_specs=(P(None, None, "stream", "wall"), P(), P(), P(), P("stream", "wall"), P(), P()),
        out_specs=P(None, None, "stream", "wall"),
        check_vma=False,
    )
```

```python
import functools
import jax
import jax.numpy as jnp
from jax import lax
from jax.experimental import pallas as pl
from jax.experimental.pallas import tpu as pltpu
from jax.sharding import PartitionSpec as P

ITERS = 2
CFL_STREAM = 0.12
RELAX = 0.3
PENALTY = 0.5
INLET_SPEED = 0.5
MESH = pl.DeviceIdType.MESH
F32 = jnp.float32
BF16 = jnp.bfloat16
NT = (((1,), (1,)), ((), ()))
TN = (((0,), (0,)), ((), ()))


def split(value):
    high = value.astype(BF16)
    return high, (value - high.astype(F32)).astype(BF16)


def kernel(
    groups, nx, ns, n_wall, n_stream,
    dist, qw_in, vx_in, vy_in, flags_in, inv_in, lc_in,
    out,
    qw, vx, vy, lc, flags, inv, sel, near, pull_l, pull_r,
    cur, rhs, packed, weight, end_row, spike, factor, ex, tx, rx, ix, ry, eya,
    edge_l, edge_r, halo_l, halo_r, ends, others, before,
    table_sem, ns_sem, nr_sem, load_sem, sl_sem, sr_sem, rl_sem, rr_sem, ws_sem, wr_sem,
):
    cw = cur.shape[1]
    half = groups // 2
    rows = nx * ns
    part = ends.shape[3]
    pieces = rows // part
    wall = lax.axis_index("wall")
    stream = lax.axis_index("stream")
    left = lax.rem(stream + n_stream - 1, n_stream)
    right = lax.rem(stream + 1, n_stream)

    loads = [
        pltpu.make_async_copy(
            dist.at[pl.ds(g * rows, rows)], cur.at[pl.ds(g * rows, rows)], load_sem.at[g]
        )
        for g in range(groups)
    ]
    for load in loads:
        load.start()
    tables = [
        pltpu.make_async_copy(source, target, table_sem.at[i])
        for i, (source, target) in enumerate(
            ((qw_in, qw), (vx_in, vx), (vy_in, vy), (lc_in, lc), (flags_in, flags), (inv_in, inv))
        )
    ]
    for table in tables:
        table.start()

    barrier = pltpu.get_barrier_semaphore()
    for to in (left, right):
        pl.semaphore_signal(barrier, inc=1, device_id=(wall, to), device_id_type=MESH)
    for step in range(1, n_wall):
        to = lax.rem(wall + step, n_wall)
        pl.semaphore_signal(barrier, inc=1, device_id=(to, stream), device_id_type=MESH)
    pl.semaphore_wait(barrier, 2 + n_wall - 1)

    def halo_copies(it, g):
        here = pl.ds(g * nx, nx)
        return (
            pltpu.make_async_remote_copy(
                src_ref=edge_r.at[it, here], dst_ref=halo_l.at[it, here],
                send_sem=sr_sem.at[it, g], recv_sem=rl_sem.at[it, g],
                device_id=(wall, right), device_id_type=MESH,
            ),
            pltpu.make_async_remote_copy(
                src_ref=edge_l.at[it, here], dst_ref=halo_r.at[it, here],
                send_sem=sl_sem.at[it, g], recv_sem=rr_sem.at[it, g],
                device_id=(wall, left), device_id_type=MESH,
            ),
        )

    def send_edges(it, g):
        here = pl.ds(g * nx, nx)
        edge_r[it, here, :] = cur[pl.ds(g * rows + ns - 1, nx, stride=ns), :]
        edge_l[it, here, :] = cur[pl.ds(g * rows, nx, stride=ns), :]
        for copy in halo_copies(it, g):
            copy.start()

    for g in range(groups):
        loads[g].wait()
        send_edges(0, g)

    for table in tables:
        table.wait()
    zero = jnp.zeros((ns, cw), F32)

    def table_step(x, carry):
        v = jnp.full((ns, cw), vx[x], F32)
        rest = jnp.exp(-0.5 * (v * v))
        shifted = v - INLET_SPEED
        inlet = jnp.exp(-0.5 * (shifted * shifted))
        pull_l[pl.ds(x, 1), :] = CFL_STREAM * jnp.maximum(v[0:1, :], 0.0)
        pull_r[pl.ds(x, 1), :] = CFL_STREAM * jnp.maximum(-v[0:1, :], 0.0)
        rx[x] = rest
        ix[x] = inlet
        sums = list(carry)
        for g in range(groups):
            w = qw[g, x]
            sums[g] = sums[g] + w * rest
            sums[groups + g] = sums[groups + g] + w * inlet
        return tuple(sums)

    sums = lax.fori_loop(0, nx, table_step, (zero,) * (2 * groups), unroll=4)
    rest_sum = zero
    inlet_sum = zero
    for g in range(groups):
        v = jnp.full((ns, cw), vy[g], F32)
        factor_y = jnp.exp(-0.5 * (v * v))
        ry[g] = factor_y
        rest_sum = rest_sum + factor_y * sums[g]
        inlet_sum = inlet_sum + factor_y * sums[groups + g]
    kind = flags[...]
    solid = jnp.where(kind == 1, PENALTY, 0.0).astype(F32)
    inflow = jnp.where(kind == 2, PENALTY, 0.0).astype(F32)
    keep = 1.0 - solid - inflow
    solid_part = solid / rest_sum
    inlet_part = inflow / inlet_sum

    row16 = lax.broadcasted_iota(jnp.int32, (16, cw), 0)
    for g in range(groups):
        m = inv[g]
        mt = m.T
        high, low = split(mt)
        weight[g, 0:cw, 0:cw] = high
        weight[g, cw:, 0:cw] = high
        weight[g, 0:cw, cw:] = low
        weight[g, cw:, cw:] = jnp.zeros((cw, cw), BF16)
        down = g < half
        last = m[cw - 1 : cw, :] if down else m[0:1, :]
        col = (mt[0:1, :] if down else mt[cw - 1 : cw, :]) * lc[g]
        last_high, last_low = split(last)
        last_high = last_high.astype(F32)
        last_low = last_low.astype(F32)
        end_row[g, :, 0:cw] = jnp.where(
            row16 == 0, last_high, jnp.where(row16 == 1, last_low, 0.0)
        ).astype(BF16)
        end_row[g, :, cw:] = jnp.where(row16 == 0, last_high, 0.0).astype(BF16)
        col_high, col_low = split(col)
        row8 = lax.broadcasted_iota(jnp.int32, (8, cw), 0)
        spike[g] = jnp.where(
            row8 < 2, col_high.astype(F32), jnp.where(row8 == 2, col_low.astype(F32), 0.0)
        )
        one = col[:, cw - 1 : cw] if down else col[:, 0:1]
        side, gg = (0, g) if down else (1, g - half)
        for h in range(pieces):
            factor[side, gg * pieces + h : gg * pieces + h + 1, :] = jnp.broadcast_to(one, (1, part))

    lane = lax.broadcasted_iota(jnp.int32, (part, nx), 0)
    line = lax.broadcasted_iota(jnp.int32, (part, nx), 1)
    for way, node in enumerate((ns - 1, 0)):
        for h in range(pieces):
            wanted = (line * ns + node) == (lane + h * part)
            sel[way, h] = jnp.where(wanted, 1.0, 0.0).astype(BF16)
    row8n = lax.broadcasted_iota(jnp.int32, (8, nx), 0)

    def near_copies():
        return [
            pltpu.make_async_remote_copy(
                src_ref=before, dst_ref=near.at[way],
                send_sem=ns_sem.at[way], recv_sem=nr_sem.at[way],
                device_id=(wall, to), device_id_type=MESH,
            )
            for way, to in enumerate((right, left))
        ]

    sub = lax.broadcasted_iota(jnp.int32, (ns, cw), 0)
    row8b = lax.broadcasted_iota(jnp.int32, (8, rows), 0)

    for it in range(ITERS):
        def moment_step(x, carry):
            sums = list(carry)
            total = None
            for g in range(groups):
                f = cur[pl.ds(pl.multiple_of(g * rows + x * ns, ns), ns), :]
                wf = qw[g, x] * f
                sums[g] = sums[g] + wf
                total = wf if total is None else total + wf
            sums[groups] = sums[groups] + vx[x] * total
            return tuple(sums)

        sums = lax.fori_loop(0, nx, moment_step, (zero,) * (groups + 1), unroll=8)
        density = sums[0]
        along_y = vy[0] * sums[0]
        for g in range(1, groups):
            density = density + sums[g]
            along_y = along_y + vy[g] * sums[g]
        speed_x = sums[groups] / density
        speed_y = along_y / density
        solid_now = solid_part * density

        def equil_step(x, carry):
            diff = vx[x] - speed_x
            e = jnp.exp(-0.5 * (diff * diff))
            ex[x] = e
            tx[x] = solid_now * rx[x] + inlet_part * ix[x]
            return tuple(carry[g] + qw[g, x] * e for g in range(groups))

        sums = lax.fori_loop(0, nx, equil_step, (zero,) * groups, unroll=8)
        zsum = zero
        vertical = []
        for g in range(groups):
            diff = vy[g] - speed_y
            e = jnp.exp(-0.5 * (diff * diff))
            vertical.append(e)
            zsum = zsum + e * sums[g]
        scale = RELAX * density / zsum
        for g in range(groups):
            eya[g] = scale * vertical[g]

        def rhs_step(x, carry):
            v = vx[x]
            from_left = CFL_STREAM * jnp.maximum(v, 0.0)
            from_right = CFL_STREAM * jnp.maximum(-v, 0.0)
            stay = keep - (from_left + from_right)
            inner_left = jnp.where(sub == 0, 0.0, from_left)
            inner_right = jnp.where(sub == ns - 1, 0.0, from_right)
            e = ex[x]
            t = tx[x]
            for g in range(groups):
                here = pl.ds(pl.multiple_of(g * rows + x * ns, ns), ns)
                f = cur[here, :]
                rhs[here, :] = (
                    stay * f
                    + inner_left * pltpu.roll(f, 1, 0)
                    + inner_right * pltpu.roll(f, ns - 1, 0)
                    + eya[g] * e
                    + ry[g] * t
                )
            return carry

        lax.fori_loop(0, nx, rhs_step, 0, unroll=4)

        def wall_copy(peer, side):
            return pltpu.make_async_remote_copy(
                src_ref=ends.at[it, side], dst_ref=others.at[it, wall],
                send_sem=ws_sem.at[it, peer], recv_sem=wr_sem.at[it, wall],
                device_id=(peer, stream), device_id_type=MESH,
            )

        def wall_arrival(peer):
            return pltpu.make_async_remote_copy(
                src_ref=ends.at[it, 0], dst_ref=others.at[it, peer],
                send_sem=ws_sem.at[it, peer], recv_sem=wr_sem.at[it, peer],
                device_id=(peer, stream), device_id_type=MESH,
            )

        picks = []
        if it > 0:
            for copy in near_copies():
                copy.wait()
            for way in range(2):
                high, low = split(near[way].reshape(16, part))
                picks.append([
                    (
                        jnp.dot(high, sel[way, h], preferred_element_type=F32),
                        jnp.dot(low, sel[way, h], preferred_element_type=F32),
                    )
                    for h in range(pieces)
                ])

        def add_halo(g):
            for copy in halo_copies(it, g):
                copy.wait()
            for way, (halo, pull) in enumerate(((halo_l, pull_l), (halo_r, pull_r))):
                value = halo[it, pl.ds(g * nx, nx), :]
                if it > 0:
                    high = low = None
                    for h in range(pieces):
                        r = g * pieces + h
                        p_high = picks[way][h][0][r : r + 1, :]
                        p_low = picks[way][h][1][r : r + 1, :]
                        high = p_high if high is None else high + p_high
                        low = p_low if low is None else low + p_low
                    left_hand = jnp.where(row8n == 1, low, jnp.where(row8n < 3, high, 0.0))
                    value = value + lax.dot_general(
                        left_hand, spike[g], TN, preferred_element_type=F32
                    )
                edge = pl.ds(g * rows + (0 if way == 0 else ns - 1), nx, stride=ns)
                rhs[edge, :] = rhs[edge, :] + pull[...] * value

        for side in range(2):
            for gg in range(half):
                g = side * half + gg
                here = pl.ds(g * rows, rows)
                add_halo(g)
                high, low = split(rhs[here, :])
                packed[here, 0:cw] = high
                packed[here, cw:] = low
                two = lax.dot_general(
                    end_row[g], packed[here, :], NT, preferred_element_type=F32
                )
                end = two[0:1, :] + two[1:2, :]
                for h in range(pieces):
                    ends[it, side, gg * pieces + h : gg * pieces + h + 1, :] = end[
                        :, h * part : (h + 1) * part
                    ]
            for peer in range(n_wall):
                @pl.when((peer > wall) if side == 0 else (peer < wall))
                def _():
                    wall_copy(peer, side).start()

        for g in range(groups):
            here = pl.ds(g * rows, rows)
            two = jnp.dot(packed[here, :], weight[g], preferred_element_type=F32)
            cur[here, :] = two[:, 0:cw] + two[:, cw:]
            if it < ITERS - 1:
                send_edges(it + 1, g)

        before[...] = jnp.zeros_like(before)
        for peer in range(n_wall):
            @pl.when(peer < wall)
            def _():
                wall_arrival(peer).wait_recv()
                before[0] = factor[0] * before[0] + others[it, peer]
        for peer in reversed(range(n_wall)):
            @pl.when(peer > wall)
            def _():
                wall_arrival(peer).wait_recv()
                before[1] = factor[1] * before[1] + others[it, peer]

        if it < ITERS - 1:
            for copy in near_copies():
                copy.start()
        for g in range(groups):
            side, gg = (0, g) if g < half else (1, g - half)
            here = pl.ds(g * rows, rows)
            b = jnp.concatenate(
                [before[side, gg * pieces + h : gg * pieces + h + 1, :] for h in range(pieces)],
                axis=1,
            )
            high, low = split(b)
            high = high.astype(F32)
            low = low.astype(F32)
            left_hand = jnp.where(row8b == 1, low, jnp.where(row8b < 3, high, 0.0))
            value = cur[here, :] + lax.dot_general(
                left_hand, spike[g], TN, preferred_element_type=F32
            )
            if it == ITERS - 1:
                out[here, :] = value
            else:
                cur[here, :] = value

        for peer in range(n_wall):
            @pl.when(peer != wall)
            def _():
                wall_arrival(peer).wait_send()


def on_device(n_wall, n_stream, dist, quad_weight, vel_x, vel_y, flags, block_inverse, line_coupling):
    groups, nx, ns, cw = dist.shape
    lines = groups * nx
    total = lines * ns
    rows = nx * ns
    pieces = 8 // (groups // 2)
    part = rows // pieces
    flat = dist.reshape(total, cw)
    hbm = pl.BlockSpec(memory_space=pltpu.HBM)
    vmem = pl.BlockSpec(memory_space=pltpu.VMEM)
    result = pl.pallas_call(
        functools.partial(kernel, groups, nx, ns, n_wall, n_stream),
        out_shape=pltpu.VMEM((total, cw), F32),
        in_specs=[hbm] * 7,
        out_specs=vmem,
        scratch_shapes=[
            pltpu.SMEM((groups, nx), F32),
            pltpu.SMEM((nx,), F32),
            pltpu.SMEM((groups,), F32),
            pltpu.SMEM((groups,), F32),
            pltpu.VMEM((ns, cw), jnp.int32),
            pltpu.VMEM((groups, cw, cw), F32),
            pltpu.VMEM((2, pieces, part, nx), BF16),
            pltpu.VMEM((2, 2, 8, part), F32),
            pltpu.VMEM((nx, cw), F32),
            pltpu.VMEM((nx, cw), F32),
            pltpu.VMEM((total, cw), F32),
            pltpu.VMEM((total, cw), F32),
            pltpu.VMEM((total, 2 * cw), BF16),
            pltpu.VMEM((groups, 2 * cw, 2 * cw), BF16),
            pltpu.VMEM((groups, 16, 2 * cw), BF16),
            pltpu.VMEM((groups, 8, cw), F32),
            pltpu.VMEM((2, 8, part), F32),
            pltpu.VMEM((nx, ns, cw), F32),
            pltpu.VMEM((nx, ns, cw), F32),
            pltpu.VMEM((nx, ns, cw), F32),
            pltpu.VMEM((nx, ns, cw), F32),
            pltpu.VMEM((groups, ns, cw), F32),
            pltpu.VMEM((groups, ns, cw), F32),
            pltpu.VMEM((ITERS, lines, cw), F32),
            pltpu.VMEM((ITERS, lines, cw), F32),
            pltpu.VMEM((ITERS, lines, cw), F32),
            pltpu.VMEM((ITERS, lines, cw), F32),
            pltpu.VMEM((ITERS, 2, 8, part), F32),
            pltpu.VMEM((ITERS, n_wall, 8, part), F32),
            pltpu.VMEM((2, 8, part), F32),
            pltpu.SemaphoreType.DMA((6,)),
            pltpu.SemaphoreType.DMA((2,)),
            pltpu.SemaphoreType.DMA((2,)),
            pltpu.SemaphoreType.DMA((groups,)),
            pltpu.SemaphoreType.DMA((ITERS, groups)),
            pltpu.SemaphoreType.DMA((ITERS, groups)),
            pltpu.SemaphoreType.DMA((ITERS, groups)),
            pltpu.SemaphoreType.DMA((ITERS, groups)),
            pltpu.SemaphoreType.DMA((ITERS, n_wall)),
            pltpu.SemaphoreType.DMA((ITERS, n_wall)),
        ],
        compiler_params=pltpu.CompilerParams(
            collective_id=0, has_side_effects=True, vmem_limit_bytes=52 * 1024 * 1024
        ),
    )(flat, quad_weight, vel_x, vel_y, flags, block_inverse, line_coupling)
    return result.reshape(groups, nx, ns, cw)


def solution(mesh):
    return jax.shard_map(
        functools.partial(on_device, mesh.shape["wall"], mesh.shape["stream"]),
        mesh=mesh,
        in_specs=(P(None, None, "stream", "wall"), P(), P(), P(), P("stream", "wall"), P(), P()),
        out_specs=P(None, None, "stream", "wall"),
        check_vma=False,
    )
```
